32 devices in a mesh: az: 8 (over z, y), rg: 4 (over x, core).
Axes of the slice: x: 2, y: 2, z: 4, core: 2. Of those that a mesh axis runs over, the one named last changes fastest.
Arguments:
- echoes: bfloat16 [2, 8192, 16384], P(None, 'rg', 'az'), may hold values from -6 to 6
- replica: bfloat16 [2, 2048], replicated, may hold values from -0.125 to 0.125
- shifts: int32 [512, 8], replicated, may hold values from 0 to 16, as said below
- tap_counts: int32 [512], replicated, may hold values from 1 to 8
- interp_weights: float32 [512, 8], replicated, may hold values from -2 to 2
- fm_rates: float32 [512], replicated, may hold values from 50 to 1000
Outputs:
- focused_image: float32 [2, 8192, 16384], P(None, ('rg', 'az'))
The draws below stay inside these ranges and needn't reach their ends.
Inputs may be any that keep to these rules, and one draw needn't show every extreme that they name: `shifts`: in some range band and Doppler block the shift is 16 while that band uses all 8 taps.
All inputs are finite; a program needn't handle non-finite values.
Results may differ from the reference program's by a relative error of at most 0.0029.
Values may be sent and summed in bfloat16 or wider, within the bound.
A program may use at most 320 MiB of HBM per device.

```python
import math
import jax
import jax.numpy as jnp
from jax import lax

AZIMUTH = 16384
RANGE_BINS = 8192
CHIRP_TAPS = 2048
INTERP_TAPS = 8
MAX_SHIFT = 16
BAND_BINS = 16
DOPPLER_BLOCKS = 8
BAND_COUNT = 512
RIM_BINS = 23


def migration_tables(key):
    shift_key = jax.random.fold_in(key, 101)
    count_key = jax.random.fold_in(key, 102)
    band_key = jax.random.fold_in(key, 103)
    block_key = jax.random.fold_in(key, 104)
    shifts = jax.random.randint(shift_key, (BAND_COUNT, DOPPLER_BLOCKS), 0, MAX_SHIFT + 1, dtype=jnp.int32)
    counts = jax.random.randint(count_key, (BAND_COUNT,), 1, INTERP_TAPS + 1, dtype=jnp.int32)
    chosen_band = jax.random.randint(band_key, (), 0, BAND_COUNT, dtype=jnp.int32)
    chosen_block = jax.random.randint(block_key, (), 0, DOPPLER_BLOCKS, dtype=jnp.int32)
    shifts = shifts.at[chosen_band, chosen_block].set(MAX_SHIFT)
    counts = counts.at[chosen_band].set(INTERP_TAPS)
    return (shifts, counts)


def draw_shifts(key, part):
    return migration_tables(key)[0]


def draw_tap_counts(key, part):
    return migration_tables(key)[1]


def block_scale(own_key, dims, cuts, smallest, largest):
    def one(axis_at, blocks):
        draws = jax.random.uniform(jax.random.fold_in(jax.random.fold_in(own_key, 6), axis_at), (blocks,), jnp.float32, smallest / len(cuts), largest / len(cuts))
        return jnp.repeat(jnp.exp(draws), dims[axis_at] // blocks).reshape((-1,) + (1,) * (len(dims) - axis_at - 1))

    loudness = one(*cuts[0])
    for cut in cuts[1:]:
        loudness = loudness * one(*cut)
    return loudness


def normal_values(own_key, dims, width, reach, cuts=(), kind=jnp.bfloat16):
    loudness = block_scale(own_key, dims, cuts, -0.22, 0.18) if cuts else 1.0
    drawn = jax.random.normal(own_key, dims, jnp.float32) * width * loudness
    return jnp.minimum(jnp.maximum(drawn, -reach), reach).astype(kind)


def setup_inputs(seed: int = 0) -> dict:
    splits = jax.random.split(jax.random.key(seed), 7)
    return {
        "echoes": normal_values(splits[0], (2, RANGE_BINS, AZIMUTH), 1.0, 6.0, ((1, 4), (2, 8))),
        "replica": normal_values(splits[1], (2, CHIRP_TAPS), CHIRP_TAPS ** -0.5, 0.125),
        "shifts": draw_shifts(jax.random.fold_in(splits[6], 71), 0),
        "tap_counts": draw_tap_counts(jax.random.fold_in(splits[6], 71), 0),
        "interp_weights": normal_values(splits[4], (BAND_COUNT, INTERP_TAPS), 0.35, 2.0, (), jnp.float32),
        "fm_rates": jnp.clip(jnp.exp(jax.random.uniform(splits[5], (BAND_COUNT,), jnp.float32, math.log(50.0), math.log(1000.0))), 50.0, 1000.0),
    }


def reference(echoes, replica, shifts, tap_counts, interp_weights, fm_rates):
    padded_len = RANGE_BINS + CHIRP_TAPS
    pulse = lax.complex(replica[0].astype(jnp.float32), replica[1].astype(jnp.float32))
    kernel = jnp.conj(jnp.fft.fft(pulse, n=padded_len))
    block_lines = min(512, AZIMUTH)
    line_blocks = AZIMUTH // block_lines
    grouped = echoes.reshape(2, RANGE_BINS, line_blocks, block_lines).transpose(2, 0, 1, 3)

    def compress(line_group):
        signal = lax.complex(line_group[0].astype(jnp.float32), line_group[1].astype(jnp.float32))
        spectra = jnp.fft.fft(signal, n=padded_len, axis=0)
        correlated = jnp.fft.ifft(spectra * kernel[:, None], axis=0)[:RANGE_BINS]
        return jnp.stack([jnp.real(correlated), jnp.imag(correlated)]).astype(jnp.bfloat16)

    pieces = lax.map(compress, grouped)
    compressed = pieces.transpose(1, 2, 0, 3).reshape(2, RANGE_BINS, AZIMUTH)

    def transform(row_group):
        return jnp.fft.fft(lax.complex(row_group[0].astype(jnp.float32), row_group[1].astype(jnp.float32)), axis=-1)

    by_band = compressed.reshape(2, BAND_COUNT, BAND_BINS, AZIMUTH).transpose(1, 0, 2, 3)
    spectrum = lax.map(transform, by_band).reshape(RANGE_BINS, AZIMUTH)
    padded = jnp.concatenate([spectrum, jnp.zeros((RIM_BINS, AZIMUTH), spectrum.dtype)], axis=0)
    col_width = AZIMUTH // DOPPLER_BLOCKS
    doppler = jnp.arange(AZIMUTH, dtype=jnp.int32)
    signed = jnp.where(doppler < AZIMUTH // 2, doppler, doppler - AZIMUTH).astype(jnp.float32) / AZIMUTH
    squared = signed * signed

    def focus(band_idx):
        columns = []
        for dop_block in range(DOPPLER_BLOCKS):
            summed = jnp.zeros((BAND_BINS, col_width), spectrum.dtype)
            for tap_idx in range(INTERP_TAPS):
                row_start = (band_idx * BAND_BINS + shifts[band_idx, dop_block] + tap_idx).astype(jnp.int32)
                segment = lax.dynamic_slice(padded, (row_start, jnp.int32(dop_block * col_width)), (BAND_BINS, col_width))
                weight = jnp.where(tap_idx < tap_counts[band_idx], interp_weights[band_idx, tap_idx], 0.0)
                summed = summed + weight * segment
            columns.append(summed)
        migrated = jnp.concatenate(columns, axis=1)
        phases = math.pi * fm_rates[band_idx] * squared
        focused = migrated * lax.complex(jnp.cos(phases), -jnp.sin(phases))
        result = jnp.fft.ifft(focused, axis=-1)
        return jnp.stack([jnp.real(result), jnp.imag(result)]).astype(jnp.float32)

    images = lax.map(focus, jnp.arange(BAND_COUNT, dtype=jnp.int32))
    return images.transpose(1, 0, 2, 3).reshape(2, RANGE_BINS, AZIMUTH)
```

```python
import functools
import math

import jax
import jax.numpy as jnp
import numpy as np
from jax import lax
from jax.experimental import pallas as pl
from jax.experimental.pallas import tpu as pltpu
from jax.sharding import PartitionSpec as P

SIDE = 128
INTERP_TAPS = 8
MAX_SHIFT = 16
BAND_BINS = 16
DOPPLER_BLOCKS = 8
CHUNKS = 2
RIM_ROWS = 32
VMEM = 56 * 1024 * 1024


def transform_tables():
    k = np.arange(SIDE)
    angle = 2.0 * np.pi * ((k[:, None] * k[None, :]) % SIDE) / SIDE
    c, s = np.cos(angle), np.sin(angle)
    forward = np.block([[c, s], [-s, c]])
    inverse = np.block([[c, -s], [s, c]])
    twist = 2.0 * np.pi * (k[:, None] * k[None, :]) / (SIDE * SIDE)
    return forward, inverse, np.cos(twist), np.sin(twist)


def split_const(matrix):
    high = jnp.asarray(matrix, jnp.float32).astype(jnp.bfloat16)
    low_np = np.asarray(matrix, np.float64) - np.asarray(
        np.asarray(matrix, np.float32).astype(jnp.bfloat16), np.float64
    )
    return jnp.stack([high, jnp.asarray(low_np, jnp.float32).astype(jnp.bfloat16)])


def split_data(value):
    high = value.astype(jnp.bfloat16)
    return high, (value - high.astype(jnp.float32)).astype(jnp.bfloat16)


NN = (((1,), (0,)), ((), ()))
NT = (((1,), (1,)), ((), ()))


def mm(a, b, dims):
    return lax.dot_general(a, b, dims, preferred_element_type=jnp.float32)


def mm2(table, data, dims):
    return mm(table[0], data, dims) + mm(table[1], data, dims)


def mm3(table, value, dims):
    high, low = split_data(value)
    return mm(table[0], high, dims) + (mm(table[1], high, dims) + mm(table[0], low, dims))


def compress_kernel(chunk, block_rows, local_rows, w_ref, own_ref, rim_ref, out_ref, window):
    dest = pl.program_id(1)
    own_rows = own_ref.shape[1]

    @pl.when(dest == 0)
    def _():
        window[:, :own_rows, :] = own_ref[...]
        window[:, own_rows:, :] = rim_ref[...]

    start = pl.multiple_of(dest * local_rows + chunk * block_rows, block_rows)
    span = w_ref.shape[2]
    total = mm(w_ref[0], window[0, pl.ds(start, span), :], NN)
    total = total + mm(w_ref[1], window[1, pl.ds(start, span), :], NN)
    total = total.astype(jnp.bfloat16)
    out_ref[0, 0] = total[:block_rows]
    out_ref[0, 1] = total[block_rows:]


def compress(weights, echoes, rim, chunk, az_count, local_rows):
    range_dev, lines = echoes.shape[1], echoes.shape[2]
    taps = rim.shape[1]
    block_rows = local_rows // CHUNKS
    tile = math.gcd(512, lines)
    span = weights.shape[2]
    return pl.pallas_call(
        functools.partial(compress_kernel, chunk, block_rows, local_rows),
        out_shape=jax.ShapeDtypeStruct((az_count, 2, block_rows, lines), jnp.bfloat16),
        grid=(lines // tile, az_count),
        in_specs=[
            pl.BlockSpec(weights.shape, lambda l, j: (0, 0, 0)),
            pl.BlockSpec((2, range_dev, tile), lambda l, j: (0, 0, l)),
            pl.BlockSpec((2, taps, tile), lambda l, j: (0, 0, l)),
        ],
        out_specs=pl.BlockSpec((1, 2, block_rows, tile), lambda l, j: (j, 0, 0, l)),
        scratch_shapes=[pltpu.VMEM((2, range_dev + taps, tile), jnp.bfloat16)],
        compiler_params=pltpu.CompilerParams(vmem_limit_bytes=VMEM),
        cost_estimate=pl.CostEstimate(
            flops=8 * az_count * block_rows * span * lines,
            bytes_accessed=4 * lines * (2 * range_dev + taps),
            transcendentals=0,
        ),
        name=f"compress_{chunk}",
    )(weights, echoes, rim)


def compress_weights(replica, block_rows):
    taps = replica.shape[1]
    span = taps + block_rows

    def banded(vector):
        cycled = jnp.concatenate([vector, jnp.zeros((span + 1 - taps,), vector.dtype)])
        return jnp.tile(cycled, block_rows)[: block_rows * span].reshape(block_rows, span)

    real_rows = banded(replica[0])
    imag_rows = banded(replica[1])
    return jnp.stack(
        [
            jnp.concatenate([real_rows, -imag_rows], axis=0),
            jnp.concatenate([imag_rows, real_rows], axis=0),
        ]
    )


def forward_kernel(table_ref, cos_ref, sin_ref, in_ref, *rest):
    out_ref, data = rest[-2], rest[-1]
    az_count, _, rows, lines = in_ref.shape
    per = lines // SIDE
    for source in range(az_count):
        for c in range(2):
            piece = in_ref[source, c].astype(jnp.float32)
            data[:, c * SIDE + source * per : c * SIDE + (source + 1) * per, :] = piece.reshape(
                rows, per, SIDE
            )

    def pair(i, _):
        both = jnp.concatenate([data[2 * i], data[2 * i + 1]], axis=1).astype(jnp.bfloat16)
        first = mm2(table_ref, both, NN)
        cosine, sine = cos_ref[...], sin_ref[...]
        turned = []
        for k in range(2):
            real = first[:SIDE, k * SIDE : (k + 1) * SIDE]
            imag = first[SIDE:, k * SIDE : (k + 1) * SIDE]
            turned.append(
                jnp.concatenate(
                    [real * cosine + imag * sine, imag * cosine - real * sine], axis=1
                )
            )
        second = mm3(table_ref, jnp.concatenate(turned, axis=0), NT)
        for k in range(2):
            out_ref[0, 2 * i + k] = second[:SIDE, k * SIDE : (k + 1) * SIDE]
            out_ref[1, 2 * i + k] = second[SIDE:, k * SIDE : (k + 1) * SIDE]
        return 0

    lax.fori_loop(0, rows // 2, pair, 0, unroll=2)


def forward(tables, lines_in, held, first_block, total_rows):
    table, cosine, sine = tables
    az_count, _, rows, lines = lines_in.shape
    whole2 = lambda i: (0, 0)
    in_specs = [
        pl.BlockSpec(table.shape, lambda i: (0, 0, 0)),
        pl.BlockSpec((SIDE, SIDE), whole2),
        pl.BlockSpec((SIDE, SIDE), whole2),
        pl.BlockSpec((az_count, 2, BAND_BINS, lines), lambda i: (0, 0, i, 0)),
    ]
    operands = [table, cosine, sine, lines_in]
    aliases = {}
    if held is not None:
        in_specs.append(pl.BlockSpec(memory_space=pl.ANY))
        operands.append(held)
        aliases = {4: 0}
    return pl.pallas_call(
        forward_kernel,
        out_shape=jax.ShapeDtypeStruct((2, total_rows, SIDE, SIDE), jnp.float32),
        grid=(rows // BAND_BINS,),
        in_specs=in_specs,
        out_specs=pl.BlockSpec((2, BAND_BINS, SIDE, SIDE), lambda i: (0, first_block + i, 0, 0)),
        scratch_shapes=[pltpu.VMEM((BAND_BINS, 2 * SIDE, SIDE), jnp.float32)],
        input_output_aliases=aliases,
        compiler_params=pltpu.CompilerParams(vmem_limit_bytes=VMEM),
        cost_estimate=pl.CostEstimate(
            flops=rows * 5 * 2 * 2 * SIDE * 2 * SIDE * SIDE * 2,
            bytes_accessed=rows * SIDE * SIDE * 12,
            transcendentals=0,
        ),
        name=f"forward_at_{first_block}",
    )(*operands)


def focus_kernel(
    shift_ref, weight_ref, table_ref, cos_ref, sin_ref, pcos_ref, psin_ref,
    spec0, spec1, spec2, out_ref, window, moved, image
):
    band = pl.program_id(0)
    for k, ref in enumerate((spec0, spec1, spec2)):
        keep = BAND_BINS if k < 2 else INTERP_TAPS
        window[:, k * BAND_BINS : k * BAND_BINS + keep] = ref[:, :keep]
    deep = SIDE // DOPPLER_BLOCKS
    taps = [weight_ref[band, t] for t in range(INTERP_TAPS)]

    def block(d, _):
        shift = shift_ref[band, d]
        spot = pl.ds(pl.multiple_of(d * deep, deep), deep)
        pcos, psin = pcos_ref[0, spot, :], psin_ref[0, spot, :]
        sums = []
        for half in range(2):
            rows = BAND_BINS // 2
            parts = []
            for c in range(2):
                total = taps[0] * window[c, pl.ds(shift + half * rows, rows), spot, :]
                for t in range(1, INTERP_TAPS):
                    total = total + taps[t] * window[c, pl.ds(shift + half * rows + t, rows), spot, :]
                parts.append(total)
            real, imag = parts
            put = slice(half * rows, (half + 1) * rows)
            moved[put, spot, :] = real * pcos + imag * psin
            low = pl.ds(pl.multiple_of(SIDE + d * deep, deep), deep)
            moved[put, low, :] = imag * pcos - real * psin
        return 0

    lax.fori_loop(0, DOPPLER_BLOCKS, block, 0)

    def pair(i, _):
        both = jnp.concatenate([moved[2 * i], moved[2 * i + 1]], axis=1)
        first = mm3(table_ref, both, NN)
        cosine, sine = cos_ref[...], sin_ref[...]
        turned = []
        for k in range(2):
            real = first[:SIDE, k * SIDE : (k + 1) * SIDE]
            imag = first[SIDE:, k * SIDE : (k + 1) * SIDE]
            turned.append(
                jnp.concatenate(
                    [real * cosine - imag * sine, imag * cosine + real * sine], axis=1
                )
            )
        second = mm2(table_ref, jnp.concatenate(turned, axis=0).astype(jnp.bfloat16), NT)
        second = second * (1.0 / (SIDE * SIDE))
        for k in range(2):
            image[2 * i + k] = second[:, k * SIDE : (k + 1) * SIDE]
        return 0

    lax.fori_loop(0, BAND_BINS // 2, pair, 0, unroll=2)
    group = 16
    for c in range(2):
        for g in range(SIDE // group):
            piece = image[:, c * SIDE + g * group : c * SIDE + (g + 1) * group, :]
            out_ref[c, :, g * group * SIDE : (g + 1) * group * SIDE] = piece.reshape(
                BAND_BINS, group * SIDE
            )


def focus(shifts, weights, tables, pcos, psin, spectrum, local_rows):
    table, cosine, sine = tables
    whole2 = lambda i, *_: (0, 0)

    def part(k):
        return pl.BlockSpec((2, BAND_BINS, SIDE, SIDE), lambda i, *_: (0, i + k, 0, 0))

    phase_spec = pl.BlockSpec((1, SIDE, SIDE), lambda i, *_: (i, 0, 0))
    return pl.pallas_call(
        focus_kernel,
        out_shape=jax.ShapeDtypeStruct((2, local_rows, SIDE * SIDE), jnp.float32),
        grid_spec=pltpu.PrefetchScalarGridSpec(
            num_scalar_prefetch=2,
            grid=(local_rows // BAND_BINS,),
            in_specs=[
                pl.BlockSpec(table.shape, lambda i, *_: (0, 0, 0)),
                pl.BlockSpec((SIDE, SIDE), whole2),
                pl.BlockSpec((SIDE, SIDE), whole2),
                phase_spec,
                phase_spec,
                part(0),
                part(1),
                part(2),
            ],
            out_specs=pl.BlockSpec((2, BAND_BINS, SIDE * SIDE), lambda i, *_: (0, i, 0)),
            scratch_shapes=[
                pltpu.VMEM((2, 2 * BAND_BINS + INTERP_TAPS, SIDE, SIDE), jnp.float32),
                pltpu.VMEM((BAND_BINS, 2 * SIDE, SIDE), jnp.float32),
                pltpu.VMEM((BAND_BINS, 2 * SIDE, SIDE), jnp.float32),
            ],
        ),
        compiler_params=pltpu.CompilerParams(vmem_limit_bytes=VMEM),
        name="focus",
    )(shifts, weights, table, cosine, sine, pcos, psin, spectrum, spectrum, spectrum)


def per_device(echoes, replica, shifts, tap_counts, interp_weights, fm_rates):
    tap_total = replica.shape[1]
    range_dev = echoes.shape[1]
    az_count = lax.axis_size("az")
    rg_count = lax.axis_size("rg")
    local_rows = range_dev // az_count
    block_rows = local_rows // CHUNKS
    bands_here = local_rows // BAND_BINS
    az_pos = lax.axis_index("az")
    rg_pos = lax.axis_index("rg")

    rim = lax.ppermute(
        echoes[:, :tap_total], "rg", [(i, i - 1) for i in range(1, rg_count)]
    )
    weights = compress_weights(replica, block_rows)
    forward_m, inverse_m, twist_cos, twist_sin = transform_tables()
    cosine = jnp.asarray(twist_cos, jnp.float32)
    sine = jnp.asarray(twist_sin, jnp.float32)
    forward_tables = (split_const(forward_m), cosine, sine)
    inverse_tables = (split_const(inverse_m), cosine, sine)

    band_first = (rg_pos * range_dev + az_pos * local_rows) // BAND_BINS
    band_shift = lax.dynamic_slice_in_dim(shifts, band_first, bands_here)
    band_taps = lax.dynamic_slice_in_dim(tap_counts, band_first, bands_here)
    band_weight = lax.dynamic_slice_in_dim(interp_weights, band_first, bands_here)
    tap_index = lax.broadcasted_iota(jnp.int32, (bands_here, INTERP_TAPS), 1)
    live_weight = jnp.where(tap_index < band_taps[:, None], band_weight, 0.0)
    band_rate = lax.dynamic_slice_in_dim(fm_rates, band_first, bands_here)
    total_lines = SIDE * SIDE
    doppler = SIDE * lax.broadcasted_iota(jnp.int32, (SIDE, SIDE), 0) + lax.broadcasted_iota(
        jnp.int32, (SIDE, SIDE), 1
    )
    signed = (
        jnp.where(doppler < total_lines // 2, doppler, doppler - total_lines).astype(jnp.float32)
        / total_lines
    )
    phases = math.pi * band_rate[:, None, None] * (signed * signed)[None]
    pcos = jnp.cos(phases)
    psin = jnp.sin(phases)

    def turn(chunk):
        part = compress(weights, echoes, rim, chunk, az_count, local_rows)
        return lax.all_to_all(part, "az", split_axis=0, concat_axis=0, tiled=True)

    turned = [turn(chunk) for chunk in range(CHUNKS)]
    place = [a * rg_count + g for g in range(rg_count) for a in range(az_count)]
    beyond = lax.ppermute(
        turned[0][:, :, :RIM_ROWS], ("az", "rg"), list(zip(place[1:], place[:-1]))
    )
    total_rows = local_rows + RIM_ROWS
    step = block_rows // BAND_BINS
    spectrum = forward(forward_tables, turned[0], None, 0, total_rows)
    spectrum = forward(forward_tables, beyond, spectrum, CHUNKS * step, total_rows)
    for chunk in range(1, CHUNKS):
        spectrum = forward(forward_tables, turned[chunk], spectrum, chunk * step, total_rows)
    return focus(band_shift, live_weight, inverse_tables, pcos, psin, spectrum, local_rows)


def solution(mesh):
    return jax.shard_map(
        per_device,
        mesh=mesh,
        in_specs=(P(None, "rg", "az"), P(), P(), P(), P(), P()),
        out_specs=P(None, ("rg", "az"), None),
        check_vma=False,
    )
```
